32 devices in a mesh: groups: 2 (over y), row: 8 (over z, x), col: 2 (over core).
Axes of the slice: x: 2, y: 2, z: 4, core: 2. Of those that a mesh axis runs over, the one named last changes fastest.
Arguments:
- sketch: int32 [64, 65536], P(None, ('groups', 'row', 'col')), parts along dimension 1, may hold values from -1 to 1, as said below
- tile_row: int32 [16, 2, 64], P(('groups', 'row'), 'col'), parts along dimension 0, may hold values from 0 to 127, as said below
- tile_col: int32 [16, 2, 64], P(('groups', 'row'), 'col'), parts along dimension 0, may hold values from 0 to 127, as said below
- tile_count: int32 [16, 2], P(('groups', 'row'), 'col'), parts along dimension 0, may hold values from 32 to 64, as said below
- neighbors: int32 [16, 2, 64, 16, 256], P(('groups', 'row'), 'col'), parts along dimension 0, may hold values from 0 to 255
- weights: bfloat16 [16, 2, 64, 16, 256], P(('groups', 'row'), 'col'), parts along dimension 0, may hold values from 0.005 to 1.125
Outputs:
- solution: float32 [64, 65536], P(None, ('groups', 'row', 'col')), parts along dimension 1
- residual: float32 [64, 65536], P(None, ('groups', 'row', 'col')), parts along dimension 1
The draws below stay inside these ranges and needn't reach their ends.
There are 2 independent parts, one for each index of `groups`. The reference program is written for one: setup_inputs(seed, part) draws one part's arguments, and reference() takes and returns one part's arrays. A program takes and returns all parts, laid end to end along the dimension named above; each array names one. Nothing has to cross between parts.
Inputs may be any that keep to these rules, and one draw needn't show every extreme that they name: `sketch`: each entry is -1 or 1. `tile_row`: device (r, c) of the row and col axes holds tiles whose block row is one of its own 8 row blocks, (2 r + c) * 8 to (2 r + c + 1) * 8 - 1. Each of these row blocks has its diagonal tile in a live slot and 4 to 8 live tiles; live slots come first. `tile_col`: A tile's block column is min(tile_row + d, 127) with 0 <= d < 16. `tile_count`: some device has all 64 slots live.
All inputs are finite; a program needn't handle non-finite values.
Results may differ from the reference program's by a relative error of at most 0.0003.
Values sent between devices are 32-bit elements; how exact they have to be, the bound alone decides.
A program may use at most 128 MiB of HBM per device.

```python
import math
import jax
import jax.numpy as jnp
from jax import lax

BLK = 256
S = 64
K = 16
TPB = 8
ITERS = 2
RPD = 8
WIN = 16
TCAP = 64
NB = 128
NROWS = 32768
N_ROW = 8
N_COL = 2


def tile_pattern(key):
    key = jax.random.fold_in(key, 101)
    key_count, key_full, key_offsets = jax.random.split(key, 3)
    devices_part = N_ROW * N_COL
    total_blocks = devices_part * RPD
    per_block = jax.random.randint(key_count, (devices_part, RPD), 4, TPB + 1, dtype=jnp.int32)
    full_device = jax.random.randint(key_full, (), 0, devices_part, dtype=jnp.int32)
    per_block = jnp.where(jnp.arange(devices_part, dtype=jnp.int32)[:, None] == full_device, TPB, per_block)
    offset_keys = jax.random.split(key_offsets, total_blocks)
    shuffled = jax.vmap(lambda one_key: jax.random.permutation(one_key, WIN - 1))(offset_keys)
    offsets = jnp.concatenate([jnp.zeros((total_blocks, 1), jnp.int32), shuffled[:, :TPB - 1].astype(jnp.int32) + 1], axis=1)
    block_rows = jnp.broadcast_to(jnp.arange(total_blocks, dtype=jnp.int32)[:, None], (total_blocks, TPB))
    block_cols = jnp.minimum(block_rows + offsets, total_blocks - 1)
    vacant = (jnp.arange(TPB, dtype=jnp.int32)[None, :] >= per_block.reshape(total_blocks, 1)).astype(jnp.int32)
    vacant = vacant.reshape(devices_part, TCAP)
    ranking = jnp.argsort(vacant * TCAP + jnp.arange(TCAP, dtype=jnp.int32)[None, :], axis=1, stable=True)
    rows_sorted = jnp.take_along_axis(block_rows.reshape(devices_part, TCAP), ranking, axis=1)
    cols_sorted = jnp.take_along_axis(block_cols.reshape(devices_part, TCAP), ranking, axis=1)
    totals = jnp.sum(per_block, axis=1).astype(jnp.int32)
    return (rows_sorted.reshape(N_ROW, N_COL, TCAP), cols_sorted.reshape(N_ROW, N_COL, TCAP), totals.reshape(N_ROW, N_COL))


def draw_tile_row(key, part):
    return tile_pattern(key)[0]


def draw_tile_col(key, part):
    return tile_pattern(key)[1]


def draw_tile_count(key, part):
    return tile_pattern(key)[2]


def draw_sketch(key, part):
    key = jax.random.fold_in(key, 13)
    return 2 * jax.random.randint(key, (S, NROWS), 0, 2, dtype=jnp.int32) - 1


def draw_weights(key, part):
    key = jax.random.fold_in(key, 7)
    dims_all = (N_ROW, N_COL, TCAP, K, BLK)
    magnitude = jnp.exp(jax.random.uniform(key, dims_all, jnp.float32, math.log(0.01), math.log(0.1)))
    climb_rate = 2.0
    height = jnp.arange(N_ROW, dtype=jnp.float32).reshape(N_ROW, 1, 1, 1, 1) / (N_ROW - 1)
    return (magnitude * (1.0 + climb_rate * height)).astype(jnp.bfloat16)


def plant(result, key, smallest, top_value):
    shape = result.shape
    spot = [jax.random.randint(jax.random.fold_in(key, axis), (), 0, shape[axis]) for axis in range(len(shape))]
    result = result.at[tuple(spot)].set(smallest)
    longest = shape.index(max(shape))
    spot[longest] = (spot[longest] + 1) % shape[longest]
    return result.at[tuple(spot)].set(top_value)


def setup_inputs(seed: int = 0, part: int = 0) -> dict:
    keys = jax.random.split(jax.random.key(seed), 7)
    part_splits = jax.random.split(jax.random.fold_in(keys[6], part), 7)
    sketch = draw_sketch(jax.random.fold_in(jax.random.fold_in(keys[6], part), 71), part)
    tile_row = draw_tile_row(jax.random.fold_in(jax.random.fold_in(keys[6], part), 71), part)
    tile_col = draw_tile_col(jax.random.fold_in(jax.random.fold_in(keys[6], part), 71), part)
    tile_count = draw_tile_count(jax.random.fold_in(jax.random.fold_in(keys[6], part), 71), part)
    neighbors = plant(jax.random.randint(part_splits[4], (N_ROW, N_COL, TCAP, K, BLK), 0, BLK), jax.random.fold_in(part_splits[4], 1), 0, BLK - 1).astype(jnp.int32)
    weights = draw_weights(jax.random.fold_in(jax.random.fold_in(keys[6], part), 71), part)
    return dict(sketch=sketch, tile_row=tile_row, tile_col=tile_col, tile_count=tile_count, neighbors=neighbors, weights=weights)


ridge_term = 1.0
precise = lax.Precision.HIGHEST

def build_tiles(neighbor, weight, alive):
    amount, nearest, extent = neighbor.shape
    values = weight.astype(jnp.float32) * alive[:, None, None]
    which = jnp.broadcast_to(jnp.arange(amount, dtype=jnp.int32)[:, None, None], neighbor.shape)
    rowpos = jnp.broadcast_to(jnp.arange(extent, dtype=jnp.int32)[None, None, :], neighbor.shape)
    blank = jnp.zeros((amount, extent, extent), jnp.float32)
    return blank.at[which, rowpos, neighbor].add(values)

def column_sums(neighbor, weight, alive):
    amount, nearest, extent = neighbor.shape
    values = weight.astype(jnp.float32) * alive[:, None, None]
    which = jnp.broadcast_to(jnp.arange(amount, dtype=jnp.int32)[:, None, None], neighbor.shape)
    return jnp.zeros((amount, extent), jnp.float32).at[which, neighbor].add(values)

def reference(sketch, tile_row, tile_col, tile_count, neighbors, weights):
    devices_part = N_ROW * N_COL
    alive_all = (jnp.arange(TCAP, dtype=jnp.int32)[None, :] < tile_count.reshape(devices_part, 1)).astype(jnp.float32)
    members = (tile_row.reshape(devices_part, TCAP), tile_col.reshape(devices_part, TCAP), alive_all, neighbors.reshape(devices_part, TCAP, K, BLK), weights.reshape(devices_part, TCAP, K, BLK))

    def add_degree(running, member):
        rows_one, cols_one, alive_one, near_one, weight_one = member
        values = weight_one.astype(jnp.float32) * alive_one[:, None, None]
        running = running.at[rows_one].add(lax.optimization_barrier(jnp.sum(values, axis=1)))
        running = running.at[cols_one].add(column_sums(near_one, weight_one, alive_one))
        return (running, None)
    degree, unused = lax.scan(add_degree, jnp.zeros((NB, BLK), jnp.float32), members)
    degree = degree.reshape(NROWS)

    def graph_apply(vectors):
        blocked = vectors.reshape(S, NB, BLK)

        def visit(running, member):
            rows_one, cols_one, alive_one, near_one, weight_one = member
            dense_tiles = build_tiles(near_one, weight_one, alive_one)
            forward = jnp.einsum('tab,stb->sta', dense_tiles, blocked[:, cols_one], precision=precise)
            mirror = jnp.einsum('tab,sta->stb', dense_tiles, blocked[:, rows_one], precision=precise)
            running = running.at[:, rows_one].add(forward).at[:, cols_one].add(mirror)
            return (running, None)
        running, unused_out = lax.scan(visit, jnp.zeros((S, NB, BLK), jnp.float32), members)
        return running.reshape(S, NROWS)
    right_side = sketch.astype(jnp.float32) * jnp.sqrt(degree)[None, :]
    diagonal = degree[None, :] + ridge_term
    solution = jnp.zeros_like(right_side)
    residual = right_side
    direction = right_side
    norm_now = lax.optimization_barrier(jnp.sum(residual * residual, axis=1, keepdims=True))
    for repeat in range(ITERS):
        applied = diagonal * direction - graph_apply(direction)
        step_len = norm_now / lax.optimization_barrier(jnp.sum(direction * applied, axis=1, keepdims=True))
        solution = solution + step_len * direction
        residual = residual - step_len * applied
        norm_next = lax.optimization_barrier(jnp.sum(residual * residual, axis=1, keepdims=True))
        direction = residual + norm_next / norm_now * direction
        norm_now = norm_next
    return (solution, residual)
```

```python
import functools
import jax
import jax.numpy as jnp
from jax import lax
from jax.experimental import pallas as pl
from jax.experimental.pallas import tpu as pltpu
from jax.sharding import PartitionSpec as P

ridge_term = 1.0
build_group = 4
apply_group = 8
reach = 15
nt = (((1,), (1,)), ((), ()))
nn = (((1,), (0,)), ((), ()))


def dot(a, b, dims):
    return lax.dot_general(a, b, dims, preferred_element_type=jnp.float32)


def build_kernel(rows_ref, cols_ref, count_ref, near_ref, weight_ref, high_ref, low_ref, degree_ref):
    group, nearest, extent = near_ref.shape
    step = pl.program_id(0)

    @pl.when(step == 0)
    def _():
        degree_ref[...] = jnp.zeros_like(degree_ref)

    for member in range(group):
        slot = step * group + member

        @pl.when(slot < count_ref[0])
        def _():
            near = near_ref[member]
            weight = weight_ref[member].astype(jnp.float32)
            total = weight
            for shift in range(1, nearest):
                same = pltpu.roll(near, shift, 0) == near
                total = total + jnp.where(same, pltpu.roll(weight, shift, 0), 0.0)
            high = total.astype(jnp.bfloat16)
            low = (total - high.astype(jnp.float32)).astype(jnp.bfloat16)
            near = near.astype(jnp.float32).astype(jnp.bfloat16)
            chunk = 64
            for half in range(extent // 128):
                lanes = slice(half * 128, half * 128 + 128)
                for part in range(extent // chunk):
                    iota = (lax.broadcasted_iota(jnp.int32, (chunk, 128), 0) + part * chunk)
                    iota = iota.astype(jnp.float32).astype(jnp.bfloat16)
                    high_acc = jnp.zeros((chunk, 128), jnp.bfloat16)
                    low_acc = jnp.zeros((chunk, 128), jnp.bfloat16)
                    for k in range(nearest):
                        hit = iota == jnp.broadcast_to(near[k : k + 1, lanes], (chunk, 128))
                        high_acc = jnp.where(hit, jnp.broadcast_to(high[k : k + 1, lanes], (chunk, 128)), high_acc)
                        low_acc = jnp.where(hit, jnp.broadcast_to(low[k : k + 1, lanes], (chunk, 128)), low_acc)
                    high_ref[member, part * chunk : part * chunk + chunk, lanes] = high_acc
                    low_ref[member, part * chunk : part * chunk + chunk, lanes] = low_acc
            ones = jnp.ones((16, extent), jnp.bfloat16)
            col_sum = dot(ones, high_ref[member], nt) + dot(ones, low_ref[member], nt)
            row_sum = jnp.sum(weight, axis=0, keepdims=True)
            r = rows_ref[slot]
            c = cols_ref[slot]
            degree_ref[pl.ds(r, 1), :] += row_sum
            degree_ref[pl.ds(c, 1), :] += col_sum[0:1]


def split_into(target, value, start):
    columns, length = value.shape
    high = value.astype(jnp.bfloat16)
    low = (value - high.astype(jnp.float32)).astype(jnp.bfloat16)
    target[:columns, start : start + length] = high
    target[columns:, start : start + length] = low


def product(split_ref, block, high, low, dims):
    columns = split_ref.shape[0] // 2
    extent = high.shape[0]
    both = split_ref[:, pl.ds(pl.multiple_of(block * extent, extent), extent)]
    first = dot(both, high, dims)
    return first[:columns] + first[columns:] + dot(both[:columns], low, dims)


def add_block(out_ref, block, value):
    extent = value.shape[1]
    out_ref[:, pl.ds(pl.multiple_of(block * extent, extent), extent)] += value


def mirror_kernel(own_blocks, rows_ref, cols_ref, count_ref, vector_ref, high_ref, low_ref, out_ref, split_ref):
    group = high_ref.shape[0]
    step = pl.program_id(0)

    @pl.when(step == 0)
    def _():
        out_ref[...] = jnp.zeros_like(out_ref)
        split_into(split_ref, vector_ref[...], 0)

    for member in range(group):
        slot = step * group + member
        c = cols_ref[slot]

        @pl.when(jnp.logical_and(slot < count_ref[0], c >= own_blocks))
        def _():
            add_block(out_ref, c - own_blocks, product(split_ref, rows_ref[slot], high_ref[member], low_ref[member], nt))


def forward_kernel(own_blocks, rows_ref, cols_ref, count_ref, own_ref, next_ref, later_ref, high_ref, low_ref, out_ref, split_ref):
    group = high_ref.shape[0]
    step = pl.program_id(0)

    @pl.when(step == 0)
    def _():
        out_ref[...] = jnp.zeros_like(out_ref)
        split_into(split_ref, own_ref[...], 0)
        split_into(split_ref, next_ref[...], own_ref.shape[1])
        split_into(split_ref, later_ref[...], 2 * own_ref.shape[1])

    for member in range(group):
        slot = step * group + member
        c = cols_ref[slot]
        r = rows_ref[slot]

        @pl.when(slot < count_ref[0])
        def _():
            add_block(out_ref, r, product(split_ref, c, high_ref[member], low_ref[member], nn))

        @pl.when(jnp.logical_and(slot < count_ref[0], c < own_blocks))
        def _():
            add_block(out_ref, c, product(split_ref, r, high_ref[member], low_ref[member], nt))


def whole(shape):
    return pl.BlockSpec(shape, lambda i, *_: (0,) * len(shape))


def params():
    return pltpu.CompilerParams(vmem_limit_bytes=48 * 1024 * 1024)


def shards(sketch, tile_row, tile_col, tile_count, neighbors, weights):
    columns, piece = sketch.shape
    slots, nearest, extent = neighbors.shape[2:]
    own_blocks = piece // extent
    axes = ("row", "col")
    devices = lax.axis_size("row") * lax.axis_size("col")
    place = lax.axis_index("row") * lax.axis_size("col") + lax.axis_index("col")
    later_len = (own_blocks - 1 + reach - 2 * own_blocks + 1) * extent

    def moved(value, steps):
        return lax.ppermute(value, axes, [(d, d + steps) for d in range(devices) if 0 <= d + steps < devices])

    base = place * own_blocks
    rows = jnp.clip(tile_row.reshape(slots) - base, 0, own_blocks - 1)
    cols = jnp.clip(tile_col.reshape(slots) - base, 0, 3 * own_blocks - 1)
    count = tile_count.reshape(1)
    near = neighbors.reshape(slots, nearest, extent)
    weight = weights.reshape(slots, nearest, extent)
    signs = sketch.astype(jnp.float32)
    next_signs = moved(signs, -1)
    later_signs = moved(signs[:, :later_len], -2)

    def tiles(size, *tail):
        return pl.BlockSpec((size,) + tail, lambda i, *_: (i,) + (0,) * len(tail))

    high, low, parts = pl.pallas_call(
        build_kernel,
        grid_spec=pltpu.PrefetchScalarGridSpec(
            num_scalar_prefetch=3,
            grid=(slots // build_group,),
            in_specs=[tiles(build_group, nearest, extent)] * 2,
            out_specs=[tiles(build_group, extent, extent)] * 2 + [whole((3 * own_blocks, extent))],
        ),
        out_shape=[jax.ShapeDtypeStruct((slots, extent, extent), jnp.bfloat16)] * 2
        + [jax.ShapeDtypeStruct((3 * own_blocks, extent), jnp.float32)],
        compiler_params=params(),
        cost_estimate=pl.CostEstimate(flops=10**10, bytes_accessed=25 * 10**6, transcendentals=0),
        name="build",
    )(rows, cols, count, near, weight)
    parts = parts.reshape(3, piece)
    below = moved(parts[1:], 1)
    further = moved(parts[2:], 2)
    above = moved(parts[:2], -1)
    beyond = moved(parts[:1], -2)
    degree = parts[0] + below[0] + further[0]
    next_degree = above[0] + parts[1] + below[1]
    later_degree = beyond[0] + above[1] + parts[2]
    diagonal = degree[None, :] + ridge_term
    right_side = signs * jnp.sqrt(degree)[None, :]
    next_side = next_signs * jnp.sqrt(next_degree)[None, :]
    later_side = later_signs * jnp.sqrt(later_degree)[None, :later_len]

    def mirror(vector):
        length = piece + later_len
        return pl.pallas_call(
            functools.partial(mirror_kernel, own_blocks),
            grid_spec=pltpu.PrefetchScalarGridSpec(
                num_scalar_prefetch=3,
                grid=(slots // apply_group,),
                in_specs=[whole((columns, piece))] + [tiles(apply_group, extent, extent)] * 2,
                out_specs=whole((columns, length)),
                scratch_shapes=[pltpu.VMEM((2 * columns, piece), jnp.bfloat16)],
            ),
            out_shape=jax.ShapeDtypeStruct((columns, length), jnp.float32),
            compiler_params=params(),
            cost_estimate=pl.CostEstimate(flops=5 * 10**9, bytes_accessed=20 * 10**6, transcendentals=0),
            name="mirror",
        )(rows, cols, count, vector, high, low)

    def forward(vector, following, later):
        return pl.pallas_call(
            functools.partial(forward_kernel, own_blocks),
            grid_spec=pltpu.PrefetchScalarGridSpec(
                num_scalar_prefetch=3,
                grid=(slots // apply_group,),
                in_specs=[whole((columns, piece)), whole((columns, piece)), whole((columns, later_len))]
                + [tiles(apply_group, extent, extent)] * 2,
                out_specs=whole((columns, piece)),
                scratch_shapes=[pltpu.VMEM((2 * columns, 2 * piece + later_len), jnp.bfloat16)],
            ),
            out_shape=jax.ShapeDtypeStruct((columns, piece), jnp.float32),
            compiler_params=params(),
            cost_estimate=pl.CostEstimate(flops=5 * 10**9, bytes_accessed=20 * 10**6, transcendentals=0),
            name="forward",
        )(rows, cols, count, vector, following, later, high, low)

    def operate(vector, following, later):
        outgoing = mirror(vector)
        first = moved(outgoing[:, :piece], 1)
        second = moved(outgoing[:, piece:], 2)
        inside = forward(vector, following, later)
        second = jnp.pad(second, ((0, 0), (0, piece - later_len)))
        return diagonal * vector - (inside + first + second)

    applied = operate(right_side, next_side, later_side)
    twice = operate(applied, moved(applied, -1), moved(applied[:, :later_len], -2))
    dots = jnp.stack(
        [
            jnp.sum(right_side * right_side, axis=1),
            jnp.sum(right_side * applied, axis=1),
            jnp.sum(applied * applied, axis=1),
            jnp.sum(applied * twice, axis=1),
        ]
    )
    norm, cross, square, triple = lax.psum(dots, axes)
    first_step = norm / cross
    next_norm = norm - 2.0 * first_step * cross + first_step * first_step * square
    ratio = next_norm / norm
    energy = cross - 2.0 * first_step * square + first_step * first_step * triple
    second_step = next_norm / (energy - ratio * next_norm / first_step)
    residual = right_side - first_step[:, None] * applied
    direction = residual + ratio[:, None] * right_side
    along = applied - first_step[:, None] * twice + ratio[:, None] * applied
    solution = first_step[:, None] * right_side + second_step[:, None] * direction
    residual = residual - second_step[:, None] * along
    return (solution, residual)


def solution(mesh):
    placed = (
        P(None, ("groups", "row", "col")),
        P(("groups", "row"), "col", None),
        P(("groups", "row"), "col", None),
        P(("groups", "row"), "col"),
        P(("groups", "row"), "col", None, None, None),
        P(("groups", "row"), "col", None, None, None),
    )
    return jax.shard_map(
        shards,
        mesh=mesh,
        in_specs=placed,
        out_specs=(P(None, ("groups", "row", "col")), P(None, ("groups", "row", "col"))),
        check_vma=False,
    )
```

```python
import functools
import jax
import jax.numpy as jnp
from jax import lax
from jax.experimental import pallas as pl
from jax.experimental.pallas import tpu as pltpu
from jax.sharding import PartitionSpec as P

ridge_term = 1.0
build_group = 4
apply_group = 8
reach = 15
nt = (((1,), (1,)), ((), ()))
nn = (((1,), (0,)), ((), ()))


def dot(a, b, dims):
    return lax.dot_general(a, b, dims, preferred_element_type=jnp.float32)


def build_kernel(rows_ref, cols_ref, count_ref, near_ref, weight_ref, high_ref, low_ref, degree_ref):
    group, nearest, extent = near_ref.shape
    step = pl.program_id(0)

    @pl.when(step == 0)
    def _():
        degree_ref[...] = jnp.zeros_like(degree_ref)

    for member in range(group):
        slot = step * group + member
        alive = (slot < count_ref[0]).astype(jnp.float32)
        near = near_ref[member]
        weight = weight_ref[member].astype(jnp.float32) * alive
        total = weight
        for shift in range(1, nearest):
            same = pltpu.roll(near, shift, 0) == near
            total = total + jnp.where(same, pltpu.roll(weight, shift, 0), 0.0)
        high = total.astype(jnp.bfloat16)
        low = (total - high.astype(jnp.float32)).astype(jnp.bfloat16)
        near = near.astype(jnp.float32).astype(jnp.bfloat16)
        chunk = 64
        for half in range(extent // 128):
            lanes = slice(half * 128, half * 128 + 128)
            for part in range(extent // chunk):
                iota = lax.broadcasted_iota(jnp.int32, (chunk, 128), 0) + part * chunk
                iota = iota.astype(jnp.float32).astype(jnp.bfloat16)
                high_acc = jnp.zeros((chunk, 128), jnp.bfloat16)
                low_acc = jnp.zeros((chunk, 128), jnp.bfloat16)
                for k in range(nearest):
                    hit = iota == jnp.broadcast_to(near[k : k + 1, lanes], (chunk, 128))
                    high_acc = jnp.where(hit, jnp.broadcast_to(high[k : k + 1, lanes], (chunk, 128)), high_acc)
                    low_acc = jnp.where(hit, jnp.broadcast_to(low[k : k + 1, lanes], (chunk, 128)), low_acc)
                high_ref[member, part * chunk : part * chunk + chunk, lanes] = high_acc
                low_ref[member, part * chunk : part * chunk + chunk, lanes] = low_acc
        ones = jnp.ones((16, extent), jnp.bfloat16)
        col_sum = dot(ones, high_ref[member], nt) + dot(ones, low_ref[member], nt)
        row_sum = jnp.sum(weight, axis=0, keepdims=True)
        degree_ref[pl.ds(rows_ref[slot], 1), :] += row_sum
        degree_ref[pl.ds(cols_ref[slot], 1), :] += col_sum[0:1]


def split_into(target, value, start):
    columns, length = value.shape
    high = value.astype(jnp.bfloat16)
    low = (value - high.astype(jnp.float32)).astype(jnp.bfloat16)
    target[:columns, start : start + length] = high
    target[columns:, start : start + length] = low


def product(split_ref, block, high, low, dims):
    columns = split_ref.shape[0] // 2
    extent = high.shape[0]
    both = split_ref[:, pl.ds(pl.multiple_of(block * extent, extent), extent)]
    first = dot(both, high, dims)
    return first[:columns] + first[columns:] + dot(both[:columns], low, dims)


def add_block(out_ref, block, value):
    extent = value.shape[1]
    out_ref[:, pl.ds(pl.multiple_of(block * extent, extent), extent)] += value


def mirror_kernel(rows_ref, cols_ref, vector_ref, high_ref, low_ref, out_ref, split_ref):
    group = high_ref.shape[0]
    step = pl.program_id(0)

    @pl.when(step == 0)
    def _():
        out_ref[...] = jnp.zeros_like(out_ref)
        split_into(split_ref, vector_ref[...], 0)

    for member in range(group):
        slot = step * group + member
        add_block(out_ref, cols_ref[slot], product(split_ref, rows_ref[slot], high_ref[member], low_ref[member], nt))


def forward_kernel(rows_ref, cols_ref, own_ref, next_ref, later_ref, high_ref, low_ref, out_ref, split_ref):
    group = high_ref.shape[0]
    step = pl.program_id(0)

    @pl.when(step == 0)
    def _():
        out_ref[...] = jnp.zeros_like(out_ref)
        split_into(split_ref, own_ref[...], 0)
        split_into(split_ref, next_ref[...], own_ref.shape[1])
        split_into(split_ref, later_ref[...], 2 * own_ref.shape[1])

    for member in range(group):
        slot = step * group + member
        add_block(out_ref, rows_ref[slot], product(split_ref, cols_ref[slot], high_ref[member], low_ref[member], nn))


def position(index):
    across = lax.axis_size("col")
    return {"row": index // across, "col": index % across}


def place_of():
    return lax.axis_index("row") * lax.axis_size("col") + lax.axis_index("col")


def degree_exchange(devices, parts_ref, out_ref, below, further, above, beyond, send_sem, recv_sem):
    own = parts_ref.shape[0] // 3
    place = place_of()
    barrier = pltpu.get_barrier_semaphore()
    for steps in (1, 2, -1, -2):
        pl.semaphore_signal(
            barrier, inc=1, device_id=position((place + steps + devices) % devices), device_id_type=pl.DeviceIdType.MESH
        )
    pl.semaphore_wait(barrier, 4)
    plan = ((1, own, 2, below), (2, 2 * own, 1, further), (-1, 0, 2, above), (-2, 0, 1, beyond))
    copies = []
    for index, (steps, start, blocks, target) in enumerate(plan):
        copy = pltpu.make_async_remote_copy(
            src_ref=parts_ref.at[start : start + blocks * own],
            dst_ref=target,
            send_sem=send_sem.at[index],
            recv_sem=recv_sem.at[index],
            device_id=position((place + steps + devices) % devices),
            device_id_type=pl.DeviceIdType.MESH,
        )
        copy.start()
        copies.append(copy)
    for copy in copies:
        copy.wait()
    out_ref[0:own] = parts_ref[0:own] + below[0:own] + further[...]
    out_ref[own : 2 * own] = above[0:own] + parts_ref[own : 2 * own] + below[own : 2 * own]
    out_ref[2 * own :] = beyond[...] + above[own : 2 * own] + parts_ref[2 * own :]


def sum_kernel(devices, value_ref, out_ref, landed, send_sem, recv_sem):
    place = place_of()
    barrier = pltpu.get_barrier_semaphore()

    def greet(steps, unused):
        pl.semaphore_signal(
            barrier, inc=1, device_id=position((place + steps) % devices), device_id_type=pl.DeviceIdType.MESH
        )
        return unused

    def copy_to(steps):
        return pltpu.make_async_remote_copy(
            src_ref=value_ref,
            dst_ref=landed.at[steps],
            send_sem=send_sem.at[steps],
            recv_sem=recv_sem.at[steps],
            device_id=position((place + steps) % devices),
            device_id_type=pl.DeviceIdType.MESH,
        )

    def begin(steps, unused):
        copy_to(steps).start()
        return unused

    def finish(steps, unused):
        copy_to(steps).wait()
        return unused

    lax.fori_loop(1, devices, greet, 0)
    pl.semaphore_wait(barrier, devices - 1)
    lax.fori_loop(1, devices, begin, 0)
    lax.fori_loop(1, devices, finish, 0)
    out_ref[...] = lax.fori_loop(1, devices, lambda steps, total: total + landed[steps], value_ref[...])


def whole(shape):
    return pl.BlockSpec(shape, lambda i, *_: (0,) * len(shape))


def params():
    return pltpu.CompilerParams(vmem_limit_bytes=48 * 1024 * 1024)


def shards(sketch, tile_row, tile_col, tile_count, neighbors, weights):
    columns, piece = sketch.shape
    slots, nearest, extent = neighbors.shape[2:]
    own_blocks = piece // extent
    axes = ("row", "col")
    devices = lax.axis_size("row") * lax.axis_size("col")
    place = place_of()
    later_len = (own_blocks - 1 + reach - 2 * own_blocks + 1) * extent

    def moved(value, steps):
        return lax.ppermute(value, axes, [(d, d + steps) for d in range(devices) if 0 <= d + steps < devices])

    base = place * own_blocks
    rows = jnp.clip(tile_row.reshape(slots) - base, 0, own_blocks - 1)
    cols = jnp.clip(tile_col.reshape(slots) - base, 0, own_blocks - 1 + reach)
    count = tile_count.reshape(1)
    near = neighbors.reshape(slots, nearest, extent)
    weight = weights.reshape(slots, nearest, extent)
    signs = sketch.astype(jnp.float32)
    next_signs = moved(signs, -1)
    later_signs = moved(signs[:, :later_len], -2)

    def tiles(size, *tail):
        return pl.BlockSpec((size,) + tail, lambda i, *_: (i,) + (0,) * len(tail))

    high, low, parts = pl.pallas_call(
        build_kernel,
        grid_spec=pltpu.PrefetchScalarGridSpec(
            num_scalar_prefetch=3,
            grid=(slots // build_group,),
            in_specs=[tiles(build_group, nearest, extent)] * 2,
            out_specs=[tiles(build_group, extent, extent)] * 2 + [whole((3 * own_blocks, extent))],
        ),
        out_shape=[jax.ShapeDtypeStruct((slots, extent, extent), jnp.bfloat16)] * 2
        + [jax.ShapeDtypeStruct((3 * own_blocks, extent), jnp.float32)],
        compiler_params=params(),
        cost_estimate=pl.CostEstimate(flops=10**10, bytes_accessed=25 * 10**6, transcendentals=0),
        name="build",
    )(rows, cols, count, near, weight)
    vmem = pl.BlockSpec(memory_space=pltpu.VMEM)
    landing = [pltpu.VMEM((blocks * own_blocks, extent), jnp.float32) for blocks in (2, 1, 2, 1)]
    degrees = pl.pallas_call(
        functools.partial(degree_exchange, devices),
        out_shape=jax.ShapeDtypeStruct(parts.shape, jnp.float32),
        in_specs=[vmem],
        out_specs=vmem,
        scratch_shapes=landing + [pltpu.SemaphoreType.DMA((4,))] * 2,
        compiler_params=pltpu.CompilerParams(collective_id=1, has_side_effects=True),
        name="degrees",
    )(parts)
    degree, next_degree, later_degree = degrees.reshape(3, piece)
    diagonal = degree[None, :] + ridge_term
    right_side = signs * jnp.sqrt(degree)[None, :]
    next_side = next_signs * jnp.sqrt(next_degree)[None, :]
    later_side = later_signs * jnp.sqrt(later_degree)[None, :later_len]

    def mirror(vector):
        length = 2 * piece + later_len
        return pl.pallas_call(
            mirror_kernel,
            grid_spec=pltpu.PrefetchScalarGridSpec(
                num_scalar_prefetch=2,
                grid=(slots // apply_group,),
                in_specs=[whole((columns, piece))] + [tiles(apply_group, extent, extent)] * 2,
                out_specs=whole((columns, length)),
                scratch_shapes=[pltpu.VMEM((2 * columns, piece), jnp.bfloat16)],
            ),
            out_shape=jax.ShapeDtypeStruct((columns, length), jnp.float32),
            compiler_params=params(),
            cost_estimate=pl.CostEstimate(flops=5 * 10**9, bytes_accessed=20 * 10**6, transcendentals=0),
            name="mirror",
        )(rows, cols, vector, high, low)

    def forward(vector, following, later):
        return pl.pallas_call(
            forward_kernel,
            grid_spec=pltpu.PrefetchScalarGridSpec(
                num_scalar_prefetch=2,
                grid=(slots // apply_group,),
                in_specs=[whole((columns, piece)), whole((columns, piece)), whole((columns, later_len))]
                + [tiles(apply_group, extent, extent)] * 2,
                out_specs=whole((columns, piece)),
                scratch_shapes=[pltpu.VMEM((2 * columns, 2 * piece + later_len), jnp.bfloat16)],
            ),
            out_shape=jax.ShapeDtypeStruct((columns, piece), jnp.float32),
            compiler_params=params(),
            cost_estimate=pl.CostEstimate(flops=5 * 10**9, bytes_accessed=20 * 10**6, transcendentals=0),
            name="forward",
        )(rows, cols, vector, following, later, high, low)

    def operate(vector, following, later):
        outgoing = mirror(vector)
        first = moved(outgoing[:, piece : 2 * piece], 1)
        second = moved(outgoing[:, 2 * piece :], 2)
        inside = forward(vector, following, later)
        second = jnp.pad(second, ((0, 0), (0, piece - later_len)))
        return diagonal * vector - (inside + outgoing[:, :piece] + first + second)

    applied = operate(right_side, next_side, later_side)
    twice = operate(applied, moved(applied, -1), moved(applied[:, :later_len], -2))
    dots = jnp.stack(
        [
            jnp.sum(right_side * right_side, axis=1),
            jnp.sum(right_side * applied, axis=1),
            jnp.sum(applied * applied, axis=1),
            jnp.sum(applied * twice, axis=1),
        ]
    )
    dots = jnp.pad(dots, ((0, 4), (0, 128 - columns)))
    dots = pl.pallas_call(
        functools.partial(sum_kernel, devices),
        out_shape=jax.ShapeDtypeStruct(dots.shape, jnp.float32),
        in_specs=[vmem],
        out_specs=vmem,
        scratch_shapes=[pltpu.VMEM((devices,) + dots.shape, jnp.float32)] + [pltpu.SemaphoreType.DMA((devices,))] * 2,
        compiler_params=pltpu.CompilerParams(collective_id=2, has_side_effects=True),
        name="total",
    )(dots)
    norm, cross, square, triple = dots[:4, :columns]
    first_step = norm / cross
    next_norm = norm - 2.0 * first_step * cross + first_step * first_step * square
    ratio = next_norm / norm
    energy = cross - 2.0 * first_step * square + first_step * first_step * triple
    second_step = next_norm / (energy - ratio * next_norm / first_step)
    residual = right_side - first_step[:, None] * applied
    direction = residual + ratio[:, None] * right_side
    along = applied - first_step[:, None] * twice + ratio[:, None] * applied
    solution = first_step[:, None] * right_side + second_step[:, None] * direction
    residual = residual - second_step[:, None] * along
    return (solution, residual)


def solution(mesh):
    placed = (
        P(None, ("groups", "row", "col")),
        P(("groups", "row"), "col", None),
        P(("groups", "row"), "col", None),
        P(("groups", "row"), "col"),
        P(("groups", "row"), "col", None, None, None),
        P(("groups", "row"), "col", None, None, None),
    )
    return jax.shard_map(
        shards,
        mesh=mesh,
        in_specs=placed,
        out_specs=(P(None, ("groups", "row", "col")), P(None, ("groups", "row", "col"))),
        check_vma=False,
    )
```

```python
import functools
import jax
import jax.numpy as jnp
from jax import lax
from jax.experimental import pallas as pl
from jax.experimental.pallas import tpu as pltpu
from jax.sharding import PartitionSpec as P

ridge_term = 1.0
build_group = 16
unrolled = 4
apply_group = 16
reach = 15
nt = (((1,), (1,)), ((), ()))
nn = (((1,), (0,)), ((), ()))


def dot(a, b, dims):
    return lax.dot_general(a, b, dims, preferred_element_type=jnp.float32)


def build_kernel(rows_ref, cols_ref, count_ref, near_ref, weight_ref, high_ref, low_ref, degree_ref):
    group, nearest, extent = near_ref.shape
    step = pl.program_id(0)

    @pl.when(step == 0)
    def _():
        degree_ref[...] = jnp.zeros_like(degree_ref)

    def visit(member):
        alive = (step * group + member < count_ref[0]).astype(jnp.float32)
        near = near_ref[member]
        weight = weight_ref[member].astype(jnp.float32) * alive
        total = weight
        for shift in range(1, nearest):
            same = pltpu.roll(near, shift, 0) == near
            total = total + jnp.where(same, pltpu.roll(weight, shift, 0), 0.0)
        high = total.astype(jnp.bfloat16)
        low = (total - high.astype(jnp.float32)).astype(jnp.bfloat16)
        near = near.astype(jnp.float32).astype(jnp.bfloat16)
        chunk = 64
        for half in range(extent // 128):
            lanes = slice(half * 128, half * 128 + 128)
            for part in range(extent // chunk):
                iota = lax.broadcasted_iota(jnp.int32, (chunk, 128), 0) + part * chunk
                iota = iota.astype(jnp.float32).astype(jnp.bfloat16)
                high_acc = jnp.zeros((chunk, 128), jnp.bfloat16)
                low_acc = jnp.zeros((chunk, 128), jnp.bfloat16)
                for k in range(nearest):
                    hit = iota == jnp.broadcast_to(near[k : k + 1, lanes], (chunk, 128))
                    high_acc = jnp.where(hit, jnp.broadcast_to(high[k : k + 1, lanes], (chunk, 128)), high_acc)
                    low_acc = jnp.where(hit, jnp.broadcast_to(low[k : k + 1, lanes], (chunk, 128)), low_acc)
                high_ref[member, part * chunk : part * chunk + chunk, lanes] = high_acc
                low_ref[member, part * chunk : part * chunk + chunk, lanes] = low_acc
        return jnp.sum(weight, axis=0, keepdims=True)

    def add_degree(member, row_sum):
        slot = step * group + member
        ones = jnp.ones((16, extent), jnp.bfloat16)
        col_sum = dot(ones, high_ref[member], nt) + dot(ones, low_ref[member], nt)
        degree_ref[pl.ds(rows_ref[slot], 1), :] += row_sum
        degree_ref[pl.ds(cols_ref[slot], 1), :] += col_sum[0:1]

    @pl.loop(0, group // unrolled)
    def _(turn):
        row_sums = []
        for member in range(unrolled):
            row_sums.append(visit(turn * unrolled + member))
            if member > 0:
                add_degree(turn * unrolled + member - 1, row_sums[member - 1])
        add_degree(turn * unrolled + unrolled - 1, row_sums[-1])


def split_into(target, value, start):
    columns, length = value.shape
    high = value.astype(jnp.bfloat16)
    low = (value - high.astype(jnp.float32)).astype(jnp.bfloat16)
    target[:columns, start : start + length] = high
    target[columns:, start : start + length] = low


def product(split_ref, block, high, low, dims):
    columns = split_ref.shape[0] // 2
    extent = high.shape[0]
    both = split_ref[:, pl.ds(pl.multiple_of(block * extent, extent), extent)]
    first = dot(both, high, dims)
    return first[:columns] + first[columns:] + dot(both[:columns], low, dims)


def add_block(out_ref, block, value):
    extent = value.shape[1]
    out_ref[:, pl.ds(pl.multiple_of(block * extent, extent), extent)] += value


def mirror_kernel(rows_ref, cols_ref, vector_ref, high_ref, low_ref, own_ref, next_ref, later_ref, out_ref, split_ref):
    group = high_ref.shape[0]
    step = pl.program_id(0)
    piece = own_ref.shape[1]

    @pl.when(step == 0)
    def _():
        out_ref[...] = jnp.zeros_like(out_ref)
        split_into(split_ref, vector_ref[...], 0)

    for member in range(group):
        slot = step * group + member
        add_block(out_ref, cols_ref[slot], product(split_ref, rows_ref[slot], high_ref[member], low_ref[member], nt))

    @pl.when(step == pl.num_programs(0) - 1)
    def _():
        own_ref[...] = out_ref[:, :piece]
        next_ref[...] = out_ref[:, piece : 2 * piece]
        later_ref[...] = out_ref[:, 2 * piece :]


def forward_kernel(rows_ref, cols_ref, own_ref, next_ref, later_ref, high_ref, low_ref, out_ref, split_ref):
    group = high_ref.shape[0]
    step = pl.program_id(0)

    @pl.when(step == 0)
    def _():
        out_ref[...] = jnp.zeros_like(out_ref)
        split_into(split_ref, own_ref[...], 0)
        split_into(split_ref, next_ref[...], own_ref.shape[1])
        split_into(split_ref, later_ref[...], 2 * own_ref.shape[1])

    for member in range(group):
        slot = step * group + member
        add_block(out_ref, rows_ref[slot], product(split_ref, cols_ref[slot], high_ref[member], low_ref[member], nn))


def position(index):
    across = lax.axis_size("col")
    return {"row": index // across, "col": index % across}


def place_of():
    return lax.axis_index("row") * lax.axis_size("col") + lax.axis_index("col")


def degree_exchange(devices, parts_ref, out_ref, below, further, above, beyond, send_sem, recv_sem):
    own = parts_ref.shape[0] // 3
    place = place_of()
    barrier = pltpu.get_barrier_semaphore()
    for steps in (1, 2, -1, -2):
        pl.semaphore_signal(
            barrier, inc=1, device_id=position((place + steps + devices) % devices), device_id_type=pl.DeviceIdType.MESH
        )
    pl.semaphore_wait(barrier, 4)
    plan = ((1, own, 2, below), (2, 2 * own, 1, further), (-1, 0, 2, above), (-2, 0, 1, beyond))
    copies = []
    for index, (steps, start, blocks, target) in enumerate(plan):
        copy = pltpu.make_async_remote_copy(
            src_ref=parts_ref.at[start : start + blocks * own],
            dst_ref=target,
            send_sem=send_sem.at[index],
            recv_sem=recv_sem.at[index],
            device_id=position((place + steps + devices) % devices),
            device_id_type=pl.DeviceIdType.MESH,
        )
        copy.start()
        copies.append(copy)
    for copy in copies:
        copy.wait()
    out_ref[0:own] = parts_ref[0:own] + below[0:own] + further[...]
    out_ref[own : 2 * own] = above[0:own] + parts_ref[own : 2 * own] + below[own : 2 * own]
    out_ref[2 * own :] = beyond[...] + above[own : 2 * own] + parts_ref[2 * own :]


def sum_kernel(devices, value_ref, out_ref, landed, send_sem, recv_sem):
    place = place_of()
    barrier = pltpu.get_barrier_semaphore()

    def greet(steps, unused):
        pl.semaphore_signal(
            barrier, inc=1, device_id=position((place + steps) % devices), device_id_type=pl.DeviceIdType.MESH
        )
        return unused

    def copy_to(steps):
        return pltpu.make_async_remote_copy(
            src_ref=value_ref,
            dst_ref=landed.at[steps],
            send_sem=send_sem.at[steps],
            recv_sem=recv_sem.at[steps],
            device_id=position((place + steps) % devices),
            device_id_type=pl.DeviceIdType.MESH,
        )

    def begin(steps, unused):
        copy_to(steps).start()
        return unused

    def finish(steps, unused):
        copy_to(steps).wait()
        return unused

    lax.fori_loop(1, devices, greet, 0)
    pl.semaphore_wait(barrier, devices - 1)
    lax.fori_loop(1, devices, begin, 0)
    lax.fori_loop(1, devices, finish, 0)
    out_ref[...] = lax.fori_loop(1, devices, lambda steps, total: total + landed[steps], value_ref[...])


def whole(shape):
    return pl.BlockSpec(shape, lambda i, *_: (0,) * len(shape))


def params():
    return pltpu.CompilerParams(vmem_limit_bytes=48 * 1024 * 1024)


def shards(sketch, tile_row, tile_col, tile_count, neighbors, weights):
    columns, piece = sketch.shape
    slots, nearest, extent = neighbors.shape[2:]
    own_blocks = piece // extent
    axes = ("row", "col")
    devices = lax.axis_size("row") * lax.axis_size("col")
    place = place_of()
    later_len = (own_blocks - 1 + reach - 2 * own_blocks + 1) * extent

    def moved(value, steps):
        return lax.ppermute(value, axes, [(d, d + steps) for d in range(devices) if 0 <= d + steps < devices])

    base = place * own_blocks
    rows = jnp.clip(tile_row.reshape(slots) - base, 0, own_blocks - 1)
    cols = jnp.clip(tile_col.reshape(slots) - base, 0, own_blocks - 1 + reach)
    count = tile_count.reshape(1)
    near = neighbors.reshape(slots, nearest, extent)
    weight = weights.reshape(slots, nearest, extent)
    signs = sketch.astype(jnp.float32)
    next_signs = moved(signs, -1)
    later_signs = moved(signs[:, :later_len], -2)

    def tiles(size, *tail):
        return pl.BlockSpec((size,) + tail, lambda i, *_: (i,) + (0,) * len(tail))

    high, low, parts = pl.pallas_call(
        build_kernel,
        grid_spec=pltpu.PrefetchScalarGridSpec(
            num_scalar_prefetch=3,
            grid=(slots // build_group,),
            in_specs=[tiles(build_group, nearest, extent)] * 2,
            out_specs=[tiles(build_group, extent, extent)] * 2 + [whole((3 * own_blocks, extent))],
        ),
        out_shape=[jax.ShapeDtypeStruct((slots, extent, extent), jnp.bfloat16)] * 2
        + [jax.ShapeDtypeStruct((3 * own_blocks, extent), jnp.float32)],
        compiler_params=params(),
        cost_estimate=pl.CostEstimate(flops=10**10, bytes_accessed=25 * 10**6, transcendentals=0),
        name="build",
    )(rows, cols, count, near, weight)
    vmem = pl.BlockSpec(memory_space=pltpu.VMEM)
    landing = [pltpu.VMEM((blocks * own_blocks, extent), jnp.float32) for blocks in (2, 1, 2, 1)]
    degrees = pl.pallas_call(
        functools.partial(degree_exchange, devices),
        out_shape=jax.ShapeDtypeStruct(parts.shape, jnp.float32),
        in_specs=[vmem],
        out_specs=vmem,
        scratch_shapes=landing + [pltpu.SemaphoreType.DMA((4,))] * 2,
        compiler_params=pltpu.CompilerParams(collective_id=1, has_side_effects=True),
        name="degrees",
    )(parts)
    degree, next_degree, later_degree = degrees.reshape(3, piece)
    diagonal = degree[None, :] + ridge_term
    right_side = signs * jnp.sqrt(degree)[None, :]
    next_side = next_signs * jnp.sqrt(next_degree)[None, :]
    later_side = later_signs * jnp.sqrt(later_degree)[None, :later_len]

    def mirror(vector):
        lengths = (piece, piece, later_len)
        return pl.pallas_call(
            mirror_kernel,
            grid_spec=pltpu.PrefetchScalarGridSpec(
                num_scalar_prefetch=2,
                grid=(slots // apply_group,),
                in_specs=[whole((columns, piece))] + [tiles(apply_group, extent, extent)] * 2,
                out_specs=[whole((columns, length)) for length in lengths],
                scratch_shapes=[
                    pltpu.VMEM((columns, sum(lengths)), jnp.float32),
                    pltpu.VMEM((2 * columns, piece), jnp.bfloat16),
                ],
            ),
            out_shape=[jax.ShapeDtypeStruct((columns, length), jnp.float32) for length in lengths],
            compiler_params=params(),
            cost_estimate=pl.CostEstimate(flops=5 * 10**9, bytes_accessed=20 * 10**6, transcendentals=0),
            name="mirror",
        )(rows, cols, vector, high, low)

    def forward(vector, following, later):
        return pl.pallas_call(
            forward_kernel,
            grid_spec=pltpu.PrefetchScalarGridSpec(
                num_scalar_prefetch=2,
                grid=(slots // apply_group,),
                in_specs=[whole((columns, piece)), whole((columns, piece)), whole((columns, later_len))]
                + [tiles(apply_group, extent, extent)] * 2,
                out_specs=whole((columns, piece)),
                scratch_shapes=[pltpu.VMEM((2 * columns, 2 * piece + later_len), jnp.bfloat16)],
            ),
            out_shape=jax.ShapeDtypeStruct((columns, piece), jnp.float32),
            compiler_params=params(),
            cost_estimate=pl.CostEstimate(flops=5 * 10**9, bytes_accessed=20 * 10**6, transcendentals=0),
            name="forward",
        )(rows, cols, vector, following, later, high, low)

    def operate(vector, following, later):
        kept, first, second = mirror(vector)
        first = moved(first, 1)
        second = moved(second, 2)
        inside = forward(vector, following, later)
        second = jnp.pad(second, ((0, 0), (0, piece - later_len)))
        return diagonal * vector - (inside + kept + first + second)

    applied = operate(right_side, next_side, later_side)
    twice = operate(applied, moved(applied, -1), moved(applied[:, :later_len], -2))
    dots = jnp.stack(
        [
            jnp.sum(right_side * right_side, axis=1),
            jnp.sum(right_side * applied, axis=1),
            jnp.sum(applied * applied, axis=1),
            jnp.sum(applied * twice, axis=1),
        ]
    )
    dots = jnp.pad(dots, ((0, 4), (0, 128 - columns)))
    dots = pl.pallas_call(
        functools.partial(sum_kernel, devices),
        out_shape=jax.ShapeDtypeStruct(dots.shape, jnp.float32),
        in_specs=[vmem],
        out_specs=vmem,
        scratch_shapes=[pltpu.VMEM((devices,) + dots.shape, jnp.float32)] + [pltpu.SemaphoreType.DMA((devices,))] * 2,
        compiler_params=pltpu.CompilerParams(collective_id=2, has_side_effects=True),
        name="total",
    )(dots)
    norm, cross, square, triple = dots[:4, :columns]
    first_step = norm / cross
    next_norm = norm - 2.0 * first_step * cross + first_step * first_step * square
    ratio = next_norm / norm
    energy = cross - 2.0 * first_step * square + first_step * first_step * triple
    second_step = next_norm / (energy - ratio * next_norm / first_step)
    residual = right_side - first_step[:, None] * applied
    direction = residual + ratio[:, None] * right_side
    along = applied - first_step[:, None] * twice + ratio[:, None] * applied
    solution = first_step[:, None] * right_side + second_step[:, None] * direction
    residual = residual - second_step[:, None] * along
    return (solution, residual)


def solution(mesh):
    placed = (
        P(None, ("groups", "row", "col")),
        P(("groups", "row"), "col", None),
        P(("groups", "row"), "col", None),
        P(("groups", "row"), "col"),
        P(("groups", "row"), "col", None, None, None),
        P(("groups", "row"), "col", None, None, None),
    )
    return jax.shard_map(
        shards,
        mesh=mesh,
        in_specs=placed,
        out_specs=(P(None, ("groups", "row", "col")), P(None, ("groups", "row", "col"))),
        check_vma=False,
    )
```

```python
import functools
import jax
import jax.numpy as jnp
from jax import lax
from jax.experimental import pallas as pl
from jax.experimental.pallas import tpu as pltpu
from jax.sharding import PartitionSpec as P

ridge_term = 1.0
build_group = 16
unrolled = 4
apply_group = 16
reach = 15
nt = (((1,), (1,)), ((), ()))
nn = (((1,), (0,)), ((), ()))


def dot(a, b, dims):
    return lax.dot_general(a, b, dims, preferred_element_type=jnp.float32)


def build_kernel(rows_ref, cols_ref, count_ref, near_ref, weight_ref, high_ref, low_ref, degree_ref):
    group, nearest, extent = near_ref.shape
    step = pl.program_id(0)

    @pl.when(step == 0)
    def _():
        degree_ref[...] = jnp.zeros_like(degree_ref)

    def visit(member):
        alive = (step * group + member < count_ref[0]).astype(jnp.float32)
        near = near_ref[member]
        weight = weight_ref[member].astype(jnp.float32) * alive
        total = weight
        for shift in range(1, nearest):
            same = pltpu.roll(near, shift, 0) == near
            total = total + jnp.where(same, pltpu.roll(weight, shift, 0), 0.0)
        high = total.astype(jnp.bfloat16)
        low = (total - high.astype(jnp.float32)).astype(jnp.bfloat16)
        near = near.astype(jnp.float32).astype(jnp.bfloat16)
        chunk = 64
        for half in range(extent // 128):
            lanes = slice(half * 128, half * 128 + 128)
            for part in range(extent // chunk):
                iota = lax.broadcasted_iota(jnp.int32, (chunk, 128), 0) + part * chunk
                iota = iota.astype(jnp.float32).astype(jnp.bfloat16)
                high_acc = jnp.zeros((chunk, 128), jnp.bfloat16)
                low_acc = jnp.zeros((chunk, 128), jnp.bfloat16)
                for k in range(nearest):
                    hit = iota == jnp.broadcast_to(near[k : k + 1, lanes], (chunk, 128))
                    high_acc = jnp.where(hit, jnp.broadcast_to(high[k : k + 1, lanes], (chunk, 128)), high_acc)
                    low_acc = jnp.where(hit, jnp.broadcast_to(low[k : k + 1, lanes], (chunk, 128)), low_acc)
                high_ref[member, part * chunk : part * chunk + chunk, lanes] = high_acc
                low_ref[member, part * chunk : part * chunk + chunk, lanes] = low_acc
        return jnp.sum(weight, axis=0, keepdims=True)

    def add_degree(member, row_sum):
        slot = step * group + member
        ones = jnp.ones((16, extent), jnp.bfloat16)
        col_sum = dot(ones, high_ref[member], nt) + dot(ones, low_ref[member], nt)
        degree_ref[pl.ds(rows_ref[slot], 1), :] += row_sum
        degree_ref[pl.ds(cols_ref[slot], 1), :] += col_sum[0:1]

    @pl.loop(0, group // unrolled)
    def _(turn):
        row_sums = []
        for member in range(unrolled):
            row_sums.append(visit(turn * unrolled + member))
            if member > 0:
                add_degree(turn * unrolled + member - 1, row_sums[member - 1])
        add_degree(turn * unrolled + unrolled - 1, row_sums[-1])


def split_into(target, value, start):
    columns, length = value.shape
    high = value.astype(jnp.bfloat16)
    low = (value - high.astype(jnp.float32)).astype(jnp.bfloat16)
    target[:columns, start : start + length] = high
    target[columns:, start : start + length] = low


def product(split_ref, block, high, low, dims):
    columns = split_ref.shape[0] // 2
    extent = high.shape[0]
    both = split_ref[:, pl.ds(pl.multiple_of(block * extent, extent), extent)]
    first = dot(both, high, dims)
    return first[:columns] + first[columns:] + dot(both[:columns], low, dims)


def add_block(out_ref, block, value):
    extent = value.shape[1]
    out_ref[:, pl.ds(pl.multiple_of(block * extent, extent), extent)] += value


def mirror_kernel(rows_ref, cols_ref, vector_ref, high_ref, low_ref, own_ref, next_ref, later_ref, out_ref, split_ref):
    group = high_ref.shape[0]
    step = pl.program_id(0)
    piece = own_ref.shape[1]

    @pl.when(step == 0)
    def _():
        out_ref[...] = jnp.zeros_like(out_ref)
        split_into(split_ref, vector_ref[...], 0)

    for member in range(group):
        slot = step * group + member
        add_block(out_ref, cols_ref[slot], product(split_ref, rows_ref[slot], high_ref[member], low_ref[member], nt))

    @pl.when(step == pl.num_programs(0) - 1)
    def _():
        own_ref[...] = out_ref[:, :piece]
        next_ref[...] = out_ref[:, piece : 2 * piece]
        later_ref[...] = out_ref[:, 2 * piece :]


def forward_kernel(rows_ref, cols_ref, own_ref, next_ref, later_ref, high_ref, low_ref, out_ref, split_ref):
    group = high_ref.shape[0]
    step = pl.program_id(0)

    @pl.when(step == 0)
    def _():
        out_ref[...] = jnp.zeros_like(out_ref)
        split_into(split_ref, own_ref[...], 0)
        split_into(split_ref, next_ref[...], own_ref.shape[1])
        split_into(split_ref, later_ref[...], 2 * own_ref.shape[1])

    for member in range(group):
        slot = step * group + member
        add_block(out_ref, rows_ref[slot], product(split_ref, cols_ref[slot], high_ref[member], low_ref[member], nn))


def position(index):
    across = lax.axis_size("col")
    return {"row": index // across, "col": index % across}


def place_of():
    return lax.axis_index("row") * lax.axis_size("col") + lax.axis_index("col")


def degree_exchange(devices, parts_ref, degree_ref, own_root, next_root, later_root, below, further, above, beyond, send_sem, recv_sem):
    own = parts_ref.shape[0] // 3
    place = place_of()
    barrier = pltpu.get_barrier_semaphore()
    for steps in (1, 2, -1, -2):
        pl.semaphore_signal(
            barrier, inc=1, device_id=position((place + steps + devices) % devices), device_id_type=pl.DeviceIdType.MESH
        )
    pl.semaphore_wait(barrier, 4)
    plan = ((1, own, 2, below), (2, 2 * own, 1, further), (-1, 0, 2, above), (-2, 0, 1, beyond))
    copies = []
    for index, (steps, start, blocks, target) in enumerate(plan):
        copy = pltpu.make_async_remote_copy(
            src_ref=parts_ref.at[start : start + blocks * own],
            dst_ref=target,
            send_sem=send_sem.at[index],
            recv_sem=recv_sem.at[index],
            device_id=position((place + steps + devices) % devices),
            device_id_type=pl.DeviceIdType.MESH,
        )
        copy.start()
        copies.append(copy)
    for copy in copies:
        copy.wait()
    totals = (
        parts_ref[0:own] + below[0:own] + further[...],
        above[0:own] + parts_ref[own : 2 * own] + below[own : 2 * own],
        beyond[...] + above[own : 2 * own] + parts_ref[2 * own :],
    )
    extent = parts_ref.shape[1]
    for total, root_ref in zip(totals, (own_root, next_root, later_root)):
        root = jnp.sqrt(total)
        for block in range(root_ref.shape[1] // extent):
            root_ref[:, block * extent : (block + 1) * extent] = root[block : block + 1]
    for block in range(own):
        degree_ref[:, block * extent : (block + 1) * extent] = totals[0][block : block + 1]


def sum_kernel(devices, value_ref, out_ref, landed, send_sem, recv_sem):
    place = place_of()
    barrier = pltpu.get_barrier_semaphore()

    def greet(steps, unused):
        pl.semaphore_signal(
            barrier, inc=1, device_id=position((place + steps) % devices), device_id_type=pl.DeviceIdType.MESH
        )
        return unused

    def copy_to(steps):
        return pltpu.make_async_remote_copy(
            src_ref=value_ref,
            dst_ref=landed.at[steps],
            send_sem=send_sem.at[steps],
            recv_sem=recv_sem.at[steps],
            device_id=position((place + steps) % devices),
            device_id_type=pl.DeviceIdType.MESH,
        )

    def begin(steps, unused):
        copy_to(steps).start()
        return unused

    def finish(steps, unused):
        copy_to(steps).wait()
        return unused

    lax.fori_loop(1, devices, greet, 0)
    pl.semaphore_wait(barrier, devices - 1)
    lax.fori_loop(1, devices, begin, 0)
    lax.fori_loop(1, devices, finish, 0)
    out_ref[...] = lax.fori_loop(1, devices, lambda steps, total: total + landed[steps], value_ref[...])


def whole(shape):
    return pl.BlockSpec(shape, lambda i, *_: (0,) * len(shape))


def params():
    return pltpu.CompilerParams(vmem_limit_bytes=48 * 1024 * 1024)


def shards(sketch, tile_row, tile_col, tile_count, neighbors, weights):
    columns, piece = sketch.shape
    slots, nearest, extent = neighbors.shape[2:]
    own_blocks = piece // extent
    axes = ("row", "col")
    devices = lax.axis_size("row") * lax.axis_size("col")
    place = place_of()
    later_len = (own_blocks - 1 + reach - 2 * own_blocks + 1) * extent

    def moved(value, steps):
        return lax.ppermute(value, axes, [(d, d + steps) for d in range(devices) if 0 <= d + steps < devices])

    base = place * own_blocks
    rows = jnp.clip(tile_row.reshape(slots) - base, 0, own_blocks - 1)
    cols = jnp.clip(tile_col.reshape(slots) - base, 0, own_blocks - 1 + reach)
    count = tile_count.reshape(1)
    near = neighbors.reshape(slots, nearest, extent)
    weight = weights.reshape(slots, nearest, extent)
    next_signs = moved(sketch, -1)
    later_signs = moved(sketch[:, :later_len], -2)

    def tiles(size, *tail):
        return pl.BlockSpec((size,) + tail, lambda i, *_: (i,) + (0,) * len(tail))

    high, low, parts = pl.pallas_call(
        build_kernel,
        grid_spec=pltpu.PrefetchScalarGridSpec(
            num_scalar_prefetch=3,
            grid=(slots // build_group,),
            in_specs=[tiles(build_group, nearest, extent)] * 2,
            out_specs=[tiles(build_group, extent, extent)] * 2 + [whole((3 * own_blocks, extent))],
        ),
        out_shape=[jax.ShapeDtypeStruct((slots, extent, extent), jnp.bfloat16)] * 2
        + [jax.ShapeDtypeStruct((3 * own_blocks, extent), jnp.float32)],
        compiler_params=params(),
        cost_estimate=pl.CostEstimate(flops=10**10, bytes_accessed=25 * 10**6, transcendentals=0),
        name="build",
    )(rows, cols, count, near, weight)
    vmem = pl.BlockSpec(memory_space=pltpu.VMEM)
    landing = [pltpu.VMEM((blocks * own_blocks, extent), jnp.float32) for blocks in (2, 1, 2, 1)]
    degree, own_root, next_root, later_root = pl.pallas_call(
        functools.partial(degree_exchange, devices),
        out_shape=[jax.ShapeDtypeStruct((1, length), jnp.float32) for length in (piece, piece, piece, later_len)],
        in_specs=[vmem],
        out_specs=[vmem] * 4,
        scratch_shapes=landing + [pltpu.SemaphoreType.DMA((4,))] * 2,
        compiler_params=pltpu.CompilerParams(collective_id=1, has_side_effects=True),
        name="degrees",
    )(parts)
    diagonal = degree + ridge_term
    right_side = sketch.astype(jnp.float32) * own_root
    next_side = next_signs.astype(jnp.float32) * next_root
    later_side = later_signs.astype(jnp.float32) * later_root

    def mirror(vector):
        lengths = (piece, piece, later_len)
        return pl.pallas_call(
            mirror_kernel,
            grid_spec=pltpu.PrefetchScalarGridSpec(
                num_scalar_prefetch=2,
                grid=(slots // apply_group,),
                in_specs=[whole((columns, piece))] + [tiles(apply_group, extent, extent)] * 2,
                out_specs=[whole((columns, length)) for length in lengths],
                scratch_shapes=[
                    pltpu.VMEM((columns, sum(lengths)), jnp.float32),
                    pltpu.VMEM((2 * columns, piece), jnp.bfloat16),
                ],
            ),
            out_shape=[jax.ShapeDtypeStruct((columns, length), jnp.float32) for length in lengths],
            compiler_params=params(),
            cost_estimate=pl.CostEstimate(flops=5 * 10**9, bytes_accessed=20 * 10**6, transcendentals=0),
            name="mirror",
        )(rows, cols, vector, high, low)

    def forward(vector, following, later):
        return pl.pallas_call(
            forward_kernel,
            grid_spec=pltpu.PrefetchScalarGridSpec(
                num_scalar_prefetch=2,
                grid=(slots // apply_group,),
                in_specs=[whole((columns, piece)), whole((columns, piece)), whole((columns, later_len))]
                + [tiles(apply_group, extent, extent)] * 2,
                out_specs=whole((columns, piece)),
                scratch_shapes=[pltpu.VMEM((2 * columns, 2 * piece + later_len), jnp.bfloat16)],
            ),
            out_shape=jax.ShapeDtypeStruct((columns, piece), jnp.float32),
            compiler_params=params(),
            cost_estimate=pl.CostEstimate(flops=5 * 10**9, bytes_accessed=20 * 10**6, transcendentals=0),
            name="forward",
        )(rows, cols, vector, following, later, high, low)

    def operate(vector, following, later):
        kept, first, second = mirror(vector)
        first = moved(first, 1)
        second = moved(second, 2)
        inside = forward(vector, following, later)
        second = jnp.pad(second, ((0, 0), (0, piece - later_len)))
        return diagonal * vector - (inside + kept + first + second)

    applied = operate(right_side, next_side, later_side)
    twice = operate(applied, moved(applied, -1), moved(applied[:, :later_len], -2))
    dots = jnp.stack(
        [
            jnp.sum(right_side * right_side, axis=1),
            jnp.sum(right_side * applied, axis=1),
            jnp.sum(applied * applied, axis=1),
            jnp.sum(applied * twice, axis=1),
        ]
    )
    dots = jnp.pad(dots, ((0, 4), (0, 128 - columns)))
    dots = pl.pallas_call(
        functools.partial(sum_kernel, devices),
        out_shape=jax.ShapeDtypeStruct(dots.shape, jnp.float32),
        in_specs=[vmem],
        out_specs=vmem,
        scratch_shapes=[pltpu.VMEM((devices,) + dots.shape, jnp.float32)] + [pltpu.SemaphoreType.DMA((devices,))] * 2,
        compiler_params=pltpu.CompilerParams(collective_id=2, has_side_effects=True),
        name="total",
    )(dots)
    norm, cross, square, triple = dots[:4, :columns]
    first_step = norm / cross
    next_norm = norm - 2.0 * first_step * cross + first_step * first_step * square
    ratio = next_norm / norm
    energy = cross - 2.0 * first_step * square + first_step * first_step * triple
    second_step = next_norm / (energy - ratio * next_norm / first_step)
    residual = right_side - first_step[:, None] * applied
    direction = residual + ratio[:, None] * right_side
    along = applied - first_step[:, None] * twice + ratio[:, None] * applied
    solution = first_step[:, None] * right_side + second_step[:, None] * direction
    residual = residual - second_step[:, None] * along
    return (solution, residual)


def solution(mesh):
    placed = (
        P(None, ("groups", "row", "col")),
        P(("groups", "row"), "col", None),
        P(("groups", "row"), "col", None),
        P(("groups", "row"), "col"),
        P(("groups", "row"), "col", None, None, None),
        P(("groups", "row"), "col", None, None, None),
    )
    return jax.shard_map(
        shards,
        mesh=mesh,
        in_specs=placed,
        out_specs=(P(None, ("groups", "row", "col")), P(None, ("groups", "row", "col"))),
        check_vma=False,
    )
```

```python
import functools
import jax
import jax.numpy as jnp
from jax import lax
from jax.experimental import pallas as pl
from jax.experimental.pallas import tpu as pltpu
from jax.sharding import PartitionSpec as P

ridge_term = 1.0
build_group = 16
unrolled = 4
apply_group = 16
reach = 15
nt = (((1,), (1,)), ((), ()))
nn = (((1,), (0,)), ((), ()))


def dot(a, b, dims):
    return lax.dot_general(a, b, dims, preferred_element_type=jnp.float32)


def build_kernel(rows_ref, cols_ref, count_ref, near_ref, weight_ref, high_ref, low_ref, degree_ref):
    group, nearest, extent = near_ref.shape
    step = pl.program_id(0)

    @pl.when(step == 0)
    def _():
        degree_ref[...] = jnp.zeros_like(degree_ref)

    def visit(member):
        alive = (step * group + member < count_ref[0]).astype(jnp.float32)
        near = near_ref[member]
        weight = weight_ref[member].astype(jnp.float32) * alive
        total = weight
        for shift in range(1, nearest):
            same = pltpu.roll(near, shift, 0) == near
            total = total + jnp.where(same, pltpu.roll(weight, shift, 0), 0.0)
        high = total.astype(jnp.bfloat16)
        low = (total - high.astype(jnp.float32)).astype(jnp.bfloat16)
        near = near.astype(jnp.float32).astype(jnp.bfloat16)
        chunk = 64
        for half in range(extent // 128):
            lanes = slice(half * 128, half * 128 + 128)
            for part in range(extent // chunk):
                iota = lax.broadcasted_iota(jnp.int32, (chunk, 128), 0) + part * chunk
                iota = iota.astype(jnp.float32).astype(jnp.bfloat16)
                high_acc = jnp.zeros((chunk, 128), jnp.bfloat16)
                low_acc = jnp.zeros((chunk, 128), jnp.bfloat16)
                for k in range(nearest):
                    hit = iota == jnp.broadcast_to(near[k : k + 1, lanes], (chunk, 128))
                    high_acc = jnp.where(hit, jnp.broadcast_to(high[k : k + 1, lanes], (chunk, 128)), high_acc)
                    low_acc = jnp.where(hit, jnp.broadcast_to(low[k : k + 1, lanes], (chunk, 128)), low_acc)
                high_ref[member, part * chunk : part * chunk + chunk, lanes] = high_acc
                low_ref[member, part * chunk : part * chunk + chunk, lanes] = low_acc
        return jnp.sum(weight, axis=0, keepdims=True)

    def add_degree(member, row_sum):
        slot = step * group + member
        ones = jnp.ones((16, extent), jnp.bfloat16)
        col_sum = dot(ones, high_ref[member], nt) + dot(ones, low_ref[member], nt)
        degree_ref[pl.ds(rows_ref[slot], 1), :] += row_sum
        degree_ref[pl.ds(cols_ref[slot], 1), :] += col_sum[0:1]

    @pl.loop(0, group // unrolled)
    def _(turn):
        row_sums = []
        for member in range(unrolled):
            row_sums.append(visit(turn * unrolled + member))
            if member > 0:
                add_degree(turn * unrolled + member - 1, row_sums[member - 1])
        add_degree(turn * unrolled + unrolled - 1, row_sums[-1])


def split_into(target, value, start):
    columns, length = value.shape
    high = value.astype(jnp.bfloat16)
    low = (value - high.astype(jnp.float32)).astype(jnp.bfloat16)
    target[:columns, start : start + length] = high
    target[columns:, start : start + length] = low


def product(split_ref, block, high, low, dims):
    columns = split_ref.shape[0] // 2
    extent = high.shape[0]
    both = split_ref[:, pl.ds(pl.multiple_of(block * extent, extent), extent)]
    first = dot(both, high, dims)
    return first[:columns] + first[columns:] + dot(both[:columns], low, dims)


def add_block(out_ref, block, value):
    extent = value.shape[1]
    out_ref[:, pl.ds(pl.multiple_of(block * extent, extent), extent)] += value


def mirror_kernel(rows_ref, cols_ref, vector_ref, high_ref, low_ref, own_ref, next_ref, later_ref, out_ref, split_ref):
    group = high_ref.shape[0]
    step = pl.program_id(0)
    piece = own_ref.shape[1]

    @pl.when(step == 0)
    def _():
        out_ref[...] = jnp.zeros_like(out_ref)
        split_into(split_ref, vector_ref[...], 0)

    for member in range(group):
        slot = step * group + member
        add_block(out_ref, cols_ref[slot], product(split_ref, rows_ref[slot], high_ref[member], low_ref[member], nt))

    @pl.when(step == pl.num_programs(0) - 1)
    def _():
        own_ref[...] = out_ref[:, :piece]
        next_ref[...] = out_ref[:, piece : 2 * piece]
        later_ref[...] = out_ref[:, 2 * piece :]


def forward_kernel(rows_ref, cols_ref, own_ref, next_ref, later_ref, high_ref, low_ref, out_ref, split_ref):
    group = high_ref.shape[0]
    step = pl.program_id(0)

    @pl.when(step == 0)
    def _():
        out_ref[...] = jnp.zeros_like(out_ref)
        split_into(split_ref, own_ref[...], 0)
        split_into(split_ref, next_ref[...], own_ref.shape[1])
        split_into(split_ref, later_ref[...], 2 * own_ref.shape[1])

    for member in range(group):
        slot = step * group + member
        add_block(out_ref, rows_ref[slot], product(split_ref, cols_ref[slot], high_ref[member], low_ref[member], nn))


def position(index):
    across = lax.axis_size("col")
    return {"row": index // across, "col": index % across}


def place_of():
    return lax.axis_index("row") * lax.axis_size("col") + lax.axis_index("col")


def degree_exchange(devices, parts_ref, degree_ref, own_root, next_root, later_root, below, further, above, beyond, send_sem, recv_sem):
    own = parts_ref.shape[0] // 3
    place = place_of()
    barrier = pltpu.get_barrier_semaphore()
    for steps in (1, 2, -1, -2):
        pl.semaphore_signal(
            barrier, inc=1, device_id=position((place + steps + devices) % devices), device_id_type=pl.DeviceIdType.MESH
        )
    pl.semaphore_wait(barrier, 4)
    plan = ((1, own, 2, below), (2, 2 * own, 1, further), (-1, 0, 2, above), (-2, 0, 1, beyond))
    copies = []
    for index, (steps, start, blocks, target) in enumerate(plan):
        copy = pltpu.make_async_remote_copy(
            src_ref=parts_ref.at[start : start + blocks * own],
            dst_ref=target,
            send_sem=send_sem.at[index],
            recv_sem=recv_sem.at[index],
            device_id=position((place + steps + devices) % devices),
            device_id_type=pl.DeviceIdType.MESH,
        )
        copy.start()
        copies.append(copy)
    for copy in copies:
        copy.wait()
    totals = (
        parts_ref[0:own] + below[0:own] + further[...],
        above[0:own] + parts_ref[own : 2 * own] + below[own : 2 * own],
        beyond[...] + above[own : 2 * own] + parts_ref[2 * own :],
    )
    extent = parts_ref.shape[1]
    for total, root_ref in zip(totals, (own_root, next_root, later_root)):
        root = jnp.sqrt(total)
        for block in range(root_ref.shape[1] // extent):
            root_ref[:, block * extent : (block + 1) * extent] = root[block : block + 1]
    for block in range(own):
        degree_ref[:, block * extent : (block + 1) * extent] = totals[0][block : block + 1]


def sum_kernel(devices, value_ref, out_ref, landed, send_sem, recv_sem):
    place = place_of()
    barrier = pltpu.get_barrier_semaphore()

    def greet(steps, unused):
        pl.semaphore_signal(
            barrier, inc=1, device_id=position((place + steps) % devices), device_id_type=pl.DeviceIdType.MESH
        )
        return unused

    def copy_to(steps):
        return pltpu.make_async_remote_copy(
            src_ref=value_ref,
            dst_ref=landed.at[steps],
            send_sem=send_sem.at[steps],
            recv_sem=recv_sem.at[steps],
            device_id=position((place + steps) % devices),
            device_id_type=pl.DeviceIdType.MESH,
        )

    def begin(steps, unused):
        copy_to(steps).start()
        return unused

    def finish(steps, unused):
        copy_to(steps).wait()
        return unused

    lax.fori_loop(1, devices, greet, 0)
    pl.semaphore_wait(barrier, devices - 1)
    lax.fori_loop(1, devices, begin, 0)
    lax.fori_loop(1, devices, finish, 0)
    out_ref[...] = lax.fori_loop(1, devices, lambda steps, total: total + landed[steps], value_ref[...])


def whole(shape):
    return pl.BlockSpec(shape, lambda i, *_: (0,) * len(shape))


def params():
    return pltpu.CompilerParams(vmem_limit_bytes=48 * 1024 * 1024)


def shards(sketch, tile_row, tile_col, tile_count, neighbors, weights):
    columns, piece = sketch.shape
    slots, nearest, extent = neighbors.shape[2:]
    own_blocks = piece // extent
    axes = ("row", "col")
    devices = lax.axis_size("row") * lax.axis_size("col")
    place = place_of()
    later_len = (own_blocks - 1 + reach - 2 * own_blocks + 1) * extent

    def moved(value, steps):
        return lax.ppermute(value, axes, [(d, d + steps) for d in range(devices) if 0 <= d + steps < devices])

    base = place * own_blocks
    rows = jnp.clip(tile_row.reshape(slots) - base, 0, own_blocks - 1)
    cols = jnp.clip(tile_col.reshape(slots) - base, 0, own_blocks - 1 + reach)
    count = tile_count.reshape(1)
    near = neighbors.reshape(slots, nearest, extent)
    weight = weights.reshape(slots, nearest, extent)
    signs = sketch.astype(jnp.float32)
    next_signs = moved(signs, -1)
    later_signs = moved(signs[:, :later_len], -2)

    def tiles(size, *tail):
        return pl.BlockSpec((size,) + tail, lambda i, *_: (i,) + (0,) * len(tail))

    high, low, parts = pl.pallas_call(
        build_kernel,
        grid_spec=pltpu.PrefetchScalarGridSpec(
            num_scalar_prefetch=3,
            grid=(slots // build_group,),
            in_specs=[tiles(build_group, nearest, extent)] * 2,
            out_specs=[tiles(build_group, extent, extent)] * 2 + [whole((3 * own_blocks, extent))],
        ),
        out_shape=[jax.ShapeDtypeStruct((slots, extent, extent), jnp.bfloat16)] * 2
        + [jax.ShapeDtypeStruct((3 * own_blocks, extent), jnp.float32)],
        compiler_params=params(),
        cost_estimate=pl.CostEstimate(flops=10**10, bytes_accessed=25 * 10**6, transcendentals=0),
        name="build",
    )(rows, cols, count, near, weight)
    vmem = pl.BlockSpec(memory_space=pltpu.VMEM)
    landing = [pltpu.VMEM((blocks * own_blocks, extent), jnp.float32) for blocks in (2, 1, 2, 1)]
    degree, own_root, next_root, later_root = pl.pallas_call(
        functools.partial(degree_exchange, devices),
        out_shape=[jax.ShapeDtypeStruct((1, length), jnp.float32) for length in (piece, piece, piece, later_len)],
        in_specs=[vmem],
        out_specs=[vmem] * 4,
        scratch_shapes=landing + [pltpu.SemaphoreType.DMA((4,))] * 2,
        compiler_params=pltpu.CompilerParams(collective_id=1, has_side_effects=True),
        name="degrees",
    )(parts)
    diagonal = degree + ridge_term
    right_side = signs * own_root
    next_side = next_signs * next_root
    later_side = later_signs * later_root

    def mirror(vector):
        lengths = (piece, piece, later_len)
        return pl.pallas_call(
            mirror_kernel,
            grid_spec=pltpu.PrefetchScalarGridSpec(
                num_scalar_prefetch=2,
                grid=(slots // apply_group,),
                in_specs=[whole((columns, piece))] + [tiles(apply_group, extent, extent)] * 2,
                out_specs=[whole((columns, length)) for length in lengths],
                scratch_shapes=[
                    pltpu.VMEM((columns, sum(lengths)), jnp.float32),
                    pltpu.VMEM((2 * columns, piece), jnp.bfloat16),
                ],
            ),
            out_shape=[jax.ShapeDtypeStruct((columns, length), jnp.float32) for length in lengths],
            compiler_params=params(),
            cost_estimate=pl.CostEstimate(flops=5 * 10**9, bytes_accessed=20 * 10**6, transcendentals=0),
            name="mirror",
        )(rows, cols, vector, high, low)

    def forward(vector, following, later):
        return pl.pallas_call(
            forward_kernel,
            grid_spec=pltpu.PrefetchScalarGridSpec(
                num_scalar_prefetch=2,
                grid=(slots // apply_group,),
                in_specs=[whole((columns, piece)), whole((columns, piece)), whole((columns, later_len))]
                + [tiles(apply_group, extent, extent)] * 2,
                out_specs=whole((columns, piece)),
                scratch_shapes=[pltpu.VMEM((2 * columns, 2 * piece + later_len), jnp.bfloat16)],
            ),
            out_shape=jax.ShapeDtypeStruct((columns, piece), jnp.float32),
            compiler_params=params(),
            cost_estimate=pl.CostEstimate(flops=5 * 10**9, bytes_accessed=20 * 10**6, transcendentals=0),
            name="forward",
        )(rows, cols, vector, following, later, high, low)

    def operate(vector, following, later):
        kept, first, second = mirror(vector)
        first = moved(first, 1)
        second = moved(second, 2)
        inside = forward(vector, following, later)
        second = jnp.pad(second, ((0, 0), (0, piece - later_len)))
        return diagonal * vector - (inside + kept + first + second)

    applied = operate(right_side, next_side, later_side)
    twice = operate(applied, moved(applied, -1), moved(applied[:, :later_len], -2))
    dots = jnp.stack(
        [
            jnp.sum(right_side * right_side, axis=1),
            jnp.sum(right_side * applied, axis=1),
            jnp.sum(applied * applied, axis=1),
            jnp.sum(applied * twice, axis=1),
        ]
    )
    dots = jnp.pad(dots, ((0, 4), (0, 128 - columns)))
    dots = pl.pallas_call(
        functools.partial(sum_kernel, devices),
        out_shape=jax.ShapeDtypeStruct(dots.shape, jnp.float32),
        in_specs=[vmem],
        out_specs=vmem,
        scratch_shapes=[pltpu.VMEM((devices,) + dots.shape, jnp.float32)] + [pltpu.SemaphoreType.DMA((devices,))] * 2,
        compiler_params=pltpu.CompilerParams(collective_id=2, has_side_effects=True),
        name="total",
    )(dots)
    norm, cross, square, triple = dots[:4, :columns]
    first_step = norm / cross
    next_norm = norm - 2.0 * first_step * cross + first_step * first_step * square
    ratio = next_norm / norm
    energy = cross - 2.0 * first_step * square + first_step * first_step * triple
    second_step = next_norm / (energy - ratio * next_norm / first_step)
    residual = right_side - first_step[:, None] * applied
    direction = residual + ratio[:, None] * right_side
    along = applied - first_step[:, None] * twice + ratio[:, None] * applied
    solution = first_step[:, None] * right_side + second_step[:, None] * direction
    residual = residual - second_step[:, None] * along
    return (solution, residual)


def solution(mesh):
    placed = (
        P(None, ("groups", "row", "col")),
        P(("groups", "row"), "col", None),
        P(("groups", "row"), "col", None),
        P(("groups", "row"), "col"),
        P(("groups", "row"), "col", None, None, None),
        P(("groups", "row"), "col", None, None, None),
    )
    return jax.shard_map(
        shards,
        mesh=mesh,
        in_specs=placed,
        out_specs=(P(None, ("groups", "row", "col")), P(None, ("groups", "row", "col"))),
        check_vma=False,
    )
```

```python
import functools
import jax
import jax.numpy as jnp
from jax import lax
from jax.experimental import pallas as pl
from jax.experimental.pallas import tpu as pltpu
from jax.sharding import PartitionSpec as P

ridge_term = 1.0
build_group = 16
unrolled = 4
apply_group = 16
reach = 15
nt = (((1,), (1,)), ((), ()))
nn = (((1,), (0,)), ((), ()))


def dot(a, b, dims):
    return lax.dot_general(a, b, dims, preferred_element_type=jnp.float32)


def build_kernel(rows_ref, cols_ref, count_ref, near_ref, weight_ref, high_ref, low_ref, degree_ref):
    group, nearest, extent = near_ref.shape
    step = pl.program_id(0)

    @pl.when(step == 0)
    def _():
        degree_ref[...] = jnp.zeros_like(degree_ref)

    def visit(member):
        alive = (step * group + member < count_ref[0]).astype(jnp.float32)
        near = near_ref[member]
        weight = weight_ref[member].astype(jnp.float32) * alive
        total = weight
        for shift in range(1, nearest):
            same = pltpu.roll(near, shift, 0) == near
            total = total + jnp.where(same, pltpu.roll(weight, shift, 0), 0.0)
        high = total.astype(jnp.bfloat16)
        low = (total - high.astype(jnp.float32)).astype(jnp.bfloat16)
        near = near.astype(jnp.float32).astype(jnp.bfloat16)
        chunk = 64
        for half in range(extent // 128):
            lanes = slice(half * 128, half * 128 + 128)
            for part in range(extent // chunk):
                iota = lax.broadcasted_iota(jnp.int32, (chunk, 128), 0) + part * chunk
                iota = iota.astype(jnp.float32).astype(jnp.bfloat16)
                high_acc = jnp.zeros((chunk, 128), jnp.bfloat16)
                low_acc = jnp.zeros((chunk, 128), jnp.bfloat16)
                for k in range(nearest):
                    hit = iota == jnp.broadcast_to(near[k : k + 1, lanes], (chunk, 128))
                    high_acc = jnp.where(hit, jnp.broadcast_to(high[k : k + 1, lanes], (chunk, 128)), high_acc)
                    low_acc = jnp.where(hit, jnp.broadcast_to(low[k : k + 1, lanes], (chunk, 128)), low_acc)
                high_ref[member, part * chunk : part * chunk + chunk, lanes] = high_acc
                low_ref[member, part * chunk : part * chunk + chunk, lanes] = low_acc
        return jnp.sum(weight, axis=0, keepdims=True)

    def add_degree(member, row_sum):
        slot = step * group + member
        ones = jnp.ones((16, extent), jnp.bfloat16)
        col_sum = dot(ones, high_ref[member], nt) + dot(ones, low_ref[member], nt)
        degree_ref[pl.ds(rows_ref[slot], 1), :] += row_sum
        degree_ref[pl.ds(cols_ref[slot], 1), :] += col_sum[0:1]

    @pl.loop(0, group // unrolled)
    def _(turn):
        row_sums = []
        for member in range(unrolled):
            row_sums.append(visit(turn * unrolled + member))
            if member > 0:
                add_degree(turn * unrolled + member - 1, row_sums[member - 1])
        add_degree(turn * unrolled + unrolled - 1, row_sums[-1])


def split_into(target, value, start):
    columns, length = value.shape
    high = value.astype(jnp.bfloat16)
    low = (value - high.astype(jnp.float32)).astype(jnp.bfloat16)
    target[:columns, start : start + length] = high
    target[columns:, start : start + length] = low


def product(split_ref, block, high, low, dims):
    columns = split_ref.shape[0] // 2
    extent = high.shape[0]
    both = split_ref[:, pl.ds(pl.multiple_of(block * extent, extent), extent)]
    first = dot(both, high, dims)
    return first[:columns] + first[columns:] + dot(both[:columns], low, dims)


def add_block(out_ref, block, value):
    extent = value.shape[1]
    out_ref[:, pl.ds(pl.multiple_of(block * extent, extent), extent)] += value


def mirror_kernel(rows_ref, cols_ref, vector_ref, high_ref, low_ref, own_ref, next_ref, later_ref, out_ref, split_ref):
    group = high_ref.shape[0]
    step = pl.program_id(0)
    piece = own_ref.shape[1]

    @pl.when(step == 0)
    def _():
        out_ref[...] = jnp.zeros_like(out_ref)
        split_into(split_ref, vector_ref[...], 0)

    for member in range(group):
        slot = step * group + member
        add_block(out_ref, cols_ref[slot], product(split_ref, rows_ref[slot], high_ref[member], low_ref[member], nt))

    @pl.when(step == pl.num_programs(0) - 1)
    def _():
        own_ref[...] = out_ref[:, :piece]
        next_ref[...] = out_ref[:, piece : 2 * piece]
        later_ref[...] = out_ref[:, 2 * piece :]


def forward_kernel(rows_ref, cols_ref, own_ref, next_ref, later_ref, high_ref, low_ref, out_ref, split_ref):
    group = high_ref.shape[0]
    step = pl.program_id(0)

    @pl.when(step == 0)
    def _():
        out_ref[...] = jnp.zeros_like(out_ref)
        split_into(split_ref, own_ref[...], 0)
        split_into(split_ref, next_ref[...], own_ref.shape[1])
        split_into(split_ref, later_ref[...], 2 * own_ref.shape[1])

    for member in range(group):
        slot = step * group + member
        add_block(out_ref, rows_ref[slot], product(split_ref, cols_ref[slot], high_ref[member], low_ref[member], nn))


def position(index):
    across = lax.axis_size("col")
    return {"row": index // across, "col": index % across}


def place_of():
    return lax.axis_index("row") * lax.axis_size("col") + lax.axis_index("col")


def degree_exchange(devices, parts_ref, out_ref, below, further, above, beyond, send_sem, recv_sem):
    own = parts_ref.shape[0] // 3
    place = place_of()
    barrier = pltpu.get_barrier_semaphore()
    for steps in (1, 2, -1, -2):
        pl.semaphore_signal(
            barrier, inc=1, device_id=position((place + steps + devices) % devices), device_id_type=pl.DeviceIdType.MESH
        )
    pl.semaphore_wait(barrier, 4)
    plan = ((1, own, 2, below), (2, 2 * own, 1, further), (-1, 0, 2, above), (-2, 0, 1, beyond))
    copies = []
    for index, (steps, start, blocks, target) in enumerate(plan):
        copy = pltpu.make_async_remote_copy(
            src_ref=parts_ref.at[start : start + blocks * own],
            dst_ref=target,
            send_sem=send_sem.at[index],
            recv_sem=recv_sem.at[index],
            device_id=position((place + steps + devices) % devices),
            device_id_type=pl.DeviceIdType.MESH,
        )
        copy.start()
        copies.append(copy)
    for copy in copies:
        copy.wait()
    out_ref[0:own] = parts_ref[0:own] + below[0:own] + further[...]
    out_ref[own : 2 * own] = above[0:own] + parts_ref[own : 2 * own] + below[own : 2 * own]
    out_ref[2 * own :] = beyond[...] + above[own : 2 * own] + parts_ref[2 * own :]


def sum_kernel(devices, value_ref, out_ref, landed, send_sem, recv_sem):
    place = place_of()
    barrier = pltpu.get_barrier_semaphore()

    def greet(steps, unused):
        pl.semaphore_signal(
            barrier, inc=1, device_id=position((place + steps) % devices), device_id_type=pl.DeviceIdType.MESH
        )
        return unused

    def copy_to(steps):
        return pltpu.make_async_remote_copy(
            src_ref=value_ref,
            dst_ref=landed.at[steps],
            send_sem=send_sem.at[steps],
            recv_sem=recv_sem.at[steps],
            device_id=position((place + steps) % devices),
            device_id_type=pl.DeviceIdType.MESH,
        )

    def begin(steps, unused):
        copy_to(steps).start()
        return unused

    def finish(steps, unused):
        copy_to(steps).wait()
        return unused

    lax.fori_loop(1, devices, greet, 0)
    pl.semaphore_wait(barrier, devices - 1)
    lax.fori_loop(1, devices, begin, 0)
    lax.fori_loop(1, devices, finish, 0)
    out_ref[...] = lax.fori_loop(1, devices, lambda steps, total: total + landed[steps], value_ref[...])


def whole(shape):
    return pl.BlockSpec(shape, lambda i, *_: (0,) * len(shape))


def params():
    return pltpu.CompilerParams(vmem_limit_bytes=48 * 1024 * 1024)


def shards(sketch, tile_row, tile_col, tile_count, neighbors, weights):
    columns, piece = sketch.shape
    slots, nearest, extent = neighbors.shape[2:]
    own_blocks = piece // extent
    axes = ("row", "col")
    devices = lax.axis_size("row") * lax.axis_size("col")
    place = place_of()
    later_len = (own_blocks - 1 + reach - 2 * own_blocks + 1) * extent

    def moved(value, steps):
        return lax.ppermute(value, axes, [(d, d + steps) for d in range(devices) if 0 <= d + steps < devices])

    base = place * own_blocks
    rows = jnp.clip(tile_row.reshape(slots) - base, 0, own_blocks - 1)
    cols = jnp.clip(tile_col.reshape(slots) - base, 0, own_blocks - 1 + reach)
    count = tile_count.reshape(1)
    near = neighbors.reshape(slots, nearest, extent)
    weight = weights.reshape(slots, nearest, extent)
    signs = sketch.astype(jnp.float32)
    next_signs = moved(sketch, -1).astype(jnp.float32)
    later_signs = moved(sketch[:, :later_len], -2).astype(jnp.float32)

    def tiles(size, *tail):
        return pl.BlockSpec((size,) + tail, lambda i, *_: (i,) + (0,) * len(tail))

    high, low, parts = pl.pallas_call(
        build_kernel,
        grid_spec=pltpu.PrefetchScalarGridSpec(
            num_scalar_prefetch=3,
            grid=(slots // build_group,),
            in_specs=[tiles(build_group, nearest, extent)] * 2,
            out_specs=[tiles(build_group, extent, extent)] * 2 + [whole((3 * own_blocks, extent))],
        ),
        out_shape=[jax.ShapeDtypeStruct((slots, extent, extent), jnp.bfloat16)] * 2
        + [jax.ShapeDtypeStruct((3 * own_blocks, extent), jnp.float32)],
        compiler_params=params(),
        cost_estimate=pl.CostEstimate(flops=10**10, bytes_accessed=25 * 10**6, transcendentals=0),
        name="build",
    )(rows, cols, count, near, weight)
    vmem = pl.BlockSpec(memory_space=pltpu.VMEM)
    landing = [pltpu.VMEM((blocks * own_blocks, extent), jnp.float32) for blocks in (2, 1, 2, 1)]
    degrees = pl.pallas_call(
        functools.partial(degree_exchange, devices),
        out_shape=jax.ShapeDtypeStruct(parts.shape, jnp.float32),
        in_specs=[vmem],
        out_specs=vmem,
        scratch_shapes=landing + [pltpu.SemaphoreType.DMA((4,))] * 2,
        compiler_params=pltpu.CompilerParams(collective_id=1, has_side_effects=True),
        name="degrees",
    )(parts)
    degree, next_degree, later_degree = degrees.reshape(3, piece)
    diagonal = degree[None, :] + ridge_term
    right_side = signs * jnp.sqrt(degree)[None, :]
    next_side = next_signs * jnp.sqrt(next_degree)[None, :]
    later_side = later_signs * jnp.sqrt(later_degree)[None, :later_len]

    def mirror(vector):
        lengths = (piece, piece, later_len)
        return pl.pallas_call(
            mirror_kernel,
            grid_spec=pltpu.PrefetchScalarGridSpec(
                num_scalar_prefetch=2,
                grid=(slots // apply_group,),
                in_specs=[whole((columns, piece))] + [tiles(apply_group, extent, extent)] * 2,
                out_specs=[whole((columns, length)) for length in lengths],
                scratch_shapes=[
                    pltpu.VMEM((columns, sum(lengths)), jnp.float32),
                    pltpu.VMEM((2 * columns, piece), jnp.bfloat16),
                ],
            ),
            out_shape=[jax.ShapeDtypeStruct((columns, length), jnp.float32) for length in lengths],
            compiler_params=params(),
            cost_estimate=pl.CostEstimate(flops=5 * 10**9, bytes_accessed=20 * 10**6, transcendentals=0),
            name="mirror",
        )(rows, cols, vector, high, low)

    def forward(vector, following, later):
        return pl.pallas_call(
            forward_kernel,
            grid_spec=pltpu.PrefetchScalarGridSpec(
                num_scalar_prefetch=2,
                grid=(slots // apply_group,),
                in_specs=[whole((columns, piece)), whole((columns, piece)), whole((columns, later_len))]
                + [tiles(apply_group, extent, extent)] * 2,
                out_specs=whole((columns, piece)),
                scratch_shapes=[pltpu.VMEM((2 * columns, 2 * piece + later_len), jnp.bfloat16)],
            ),
            out_shape=jax.ShapeDtypeStruct((columns, piece), jnp.float32),
            compiler_params=params(),
            cost_estimate=pl.CostEstimate(flops=5 * 10**9, bytes_accessed=20 * 10**6, transcendentals=0),
            name="forward",
        )(rows, cols, vector, following, later, high, low)

    def operate(vector, following, later):
        kept, first, second = mirror(vector)
        first = moved(first, 1)
        second = moved(second, 2)
        inside = forward(vector, following, later)
        second = jnp.pad(second, ((0, 0), (0, piece - later_len)))
        return diagonal * vector - (inside + kept + first + second)

    applied = operate(right_side, next_side, later_side)
    twice = operate(applied, moved(applied, -1), moved(applied[:, :later_len], -2))
    dots = jnp.stack(
        [
            jnp.sum(right_side * right_side, axis=1),
            jnp.sum(right_side * applied, axis=1),
            jnp.sum(applied * applied, axis=1),
            jnp.sum(applied * twice, axis=1),
        ]
    )
    dots = jnp.pad(dots, ((0, 4), (0, 128 - columns)))
    dots = pl.pallas_call(
        functools.partial(sum_kernel, devices),
        out_shape=jax.ShapeDtypeStruct(dots.shape, jnp.float32),
        in_specs=[vmem],
        out_specs=vmem,
        scratch_shapes=[pltpu.VMEM((devices,) + dots.shape, jnp.float32)] + [pltpu.SemaphoreType.DMA((devices,))] * 2,
        compiler_params=pltpu.CompilerParams(collective_id=2, has_side_effects=True),
        name="total",
    )(dots)
    norm, cross, square, triple = dots[:4, :columns]
    first_step = norm / cross
    next_norm = norm - 2.0 * first_step * cross + first_step * first_step * square
    ratio = next_norm / norm
    energy = cross - 2.0 * first_step * square + first_step * first_step * triple
    second_step = next_norm / (energy - ratio * next_norm / first_step)
    residual = right_side - first_step[:, None] * applied
    direction = residual + ratio[:, None] * right_side
    along = applied - first_step[:, None] * twice + ratio[:, None] * applied
    solution = first_step[:, None] * right_side + second_step[:, None] * direction
    residual = residual - second_step[:, None] * along
    return (solution, residual)


def solution(mesh):
    placed = (
        P(None, ("groups", "row", "col")),
        P(("groups", "row"), "col", None),
        P(("groups", "row"), "col", None),
        P(("groups", "row"), "col"),
        P(("groups", "row"), "col", None, None, None),
        P(("groups", "row"), "col", None, None, None),
    )
    return jax.shard_map(
        shards,
        mesh=mesh,
        in_specs=placed,
        out_specs=(P(None, ("groups", "row", "col")), P(None, ("groups", "row", "col"))),
        check_vma=False,
    )
```
